1024 devices in a mesh: node: 64 (over y, z_hi, x), local: 16 (over z_lo, core).
Axes of the slice: x: 4, y: 8, z: 16 (z_hi: 2, z_lo: 8; z = z_hi * 8 + z_lo), core: 2. Of those that a mesh axis runs over, the one named last changes fastest.
Arguments:
- activations: bfloat16 [131072, 4096], P(('node', 'local')), may hold values from -24 to 24
- codes: bfloat16 [16, 256, 128], P('local'), may hold values from -127 to 127, as said below
- scales: float32 [16, 128], P('local'), may hold values from 5e-05 to 0.0005
- cotangent: bfloat16 [131072, 128], P(('node', 'local')), may hold values from -6 to 6
Outputs:
- values_out: bfloat16 [131072, 128], P(('node', 'local'))
- weight_grad: float32 [4096, 128], P(('node', 'local'))
The draws below stay inside these ranges and needn't reach their ends.
Inputs may be any that keep to these rules, and one draw needn't show every extreme that they name: codes are whole numbers.
All inputs are finite; a program needn't handle non-finite values.
Results may differ from the reference program's by a relative error of at most 0.0048.
Values may be sent and summed in bfloat16 or wider, within the bound.
No kernel may reach another device: no remote copies, remote signals or barrier semaphores. Data moves between devices by JAX's collectives and lax.ppermute only.
A program may use at most 32 MiB of HBM per device.

```python
import math
import jax
import jax.numpy as jnp
from jax import lax

D = 4096
HD = 128
BLOCK = 256
TOK_DEV = 128
BLOCKS = 16
TOKENS = 131072
N_NODE = 64
N_LOCAL = 16


def draw_codes(key, part):
    key = jax.random.fold_in(key, 11)
    whole = jax.random.randint(key, (BLOCKS, BLOCK, HD), -127, 128)
    return whole.astype(jnp.float32).astype(jnp.bfloat16)


def raised(values, rng, source, target, shards_of, factor):
    def block_of(axis_at):
        return (jnp.arange(values.shape[axis_at]) // (values.shape[axis_at] // shards_of)).reshape((-1,) + (1,) * (values.ndim - 1 - axis_at))

    near = jax.random.permutation(rng, shards_of)[block_of(target)]
    second = (block_of(target) + shards_of // 2) % shards_of
    return jnp.where((block_of(source) == near) | (block_of(source) == second), factor * values, values)


def shard_levels(rng, shape, split, smallest, top_value):
    gain, own = 1.0, jax.random.fold_in(rng, 6)
    for axis_at, shards_of in split:
        steps = jnp.exp(jax.random.uniform(jax.random.fold_in(own, axis_at), (shards_of,), jnp.float32, smallest / len(split), top_value / len(split)))
        gain = gain * jnp.repeat(steps, shape[axis_at] // shards_of).reshape([-1 if axis == axis_at else 1 for axis in range(len(shape))])
    return gain


def noise(key, shape, width, bound, shards=(), dtype=jnp.bfloat16):
    level = shard_levels(key, shape, shards, -0.22, 0.18) if shards else 1.0
    array = jax.random.normal(key, shape, jnp.float32) * width * level
    return jnp.minimum(jnp.maximum(array, -bound), bound).astype(dtype)


def heavy_noise(key, shape, spread, most, cuts, heavy, kind=jnp.bfloat16):
    values = spread * jax.random.normal(key, shape, jnp.float32)
    if cuts:
        values = values * shard_levels(key, shape, cuts, -0.22, 0.18)
    return jnp.clip(raised(values, jax.random.fold_in(key, 3), *heavy), -most, most).astype(kind)


def setup_inputs(seed: int = 0) -> dict:
    arg_keys = jax.random.split(jax.random.key(seed), 5)
    activations = heavy_noise(arg_keys[0], (TOKENS, D), 1.0, 24.0, ((0, 1024),), (0, 1, 1024, 6.0))
    codes = draw_codes(jax.random.fold_in(arg_keys[4], 71), 0)
    scales = jnp.clip(jnp.exp(math.log(0.0005) - 2.3025852 * jax.random.uniform(arg_keys[2], (BLOCKS, HD), jnp.float32) ** shard_levels(arg_keys[2], (BLOCKS, HD), ((0, 16),), -0.2, 0.2)), 4.999999873689376e-05, 0.0005)
    cotangent = noise(arg_keys[3], (TOKENS, HD), 1.0, 6.0, ((0, 1024),))
    return dict(activations=activations, codes=codes, scales=scales, cotangent=cotangent)


def dequantize(codes, scales):
    weight = codes.astype(jnp.float32) * scales[:, None, :]
    return weight.astype(jnp.bfloat16).reshape(-1, codes.shape[2])


def reference(activations, codes, scales, cotangent):
    weight = dequantize(codes, scales)
    groups = N_NODE * N_LOCAL
    act_blocks = activations.reshape(groups, TOK_DEV, D)
    cot_blocks = cotangent.reshape(groups, TOK_DEV, HD)

    def step(total, pair):
        rows, grads = pair
        values = jnp.dot(rows, weight, preferred_element_type=jnp.float32).astype(jnp.bfloat16)
        term = lax.dot_general(rows, grads, (((0,), (0,)), ((), ())), preferred_element_type=jnp.float32)
        return total + term, values

    start = jnp.zeros((D, HD), jnp.float32)
    total, values = lax.scan(step, start, (act_blocks, cot_blocks))
    weight_grad = total * (float(TOKENS) ** -0.5)
    return values.reshape(TOKENS, HD), weight_grad
```

```python
import jax
import jax.numpy as jnp
from jax import lax
from jax.experimental import pallas as pl
from jax.experimental.pallas import tpu as pltpu
from jax.sharding import Mesh, PartitionSpec as P

Y, ZH, X, ZL, CORE = 8, 2, 4, 8, 2
AXES = ("y", "zh", "x", "zl", "core")


def term_kernel(scale, core_ref, act_ref, cot_ref, keep_ref, send_ref):
    first = core_ref[0] == 0
    share = 4
    per = act_ref.shape[1] // (Y * ZH)
    sub = per // X
    half = sub // 2
    cot = cot_ref[...]
    low = lax.broadcasted_iota(jnp.int32, (sub // 16, 8, cot.shape[1]), 1) < share
    for outer in range(Y * ZH):
        part = lax.dot_general(
            act_ref[:, outer * per : (outer + 1) * per],
            cot,
            (((0,), (0,)), ((), ())),
            preferred_element_type=jnp.float32,
        )
        part = part * scale
        for x in range(X):
            tiles = part[x * sub : (x + 1) * sub].reshape(sub // 16, 2, 8, cot.shape[1])
            even, odd = tiles[:, 0], tiles[:, 1]
            zero = jnp.where(low, even, pltpu.roll(odd, share, 1))
            one = jnp.where(low, pltpu.roll(even, share, 1), odd)
            at = pl.ds((x * Y * ZH + outer) * half, half)
            keep_ref[at, :] = jnp.where(first, zero, one).reshape(half, -1)
            send_ref[at, :] = jnp.where(first, one, zero).reshape(half, -1)


def project_kernel(core_ref, act_ref, own_ref, other_ref, out_ref):
    core = core_ref[0]
    block = own_ref.shape[1]
    total = None
    for zl in range(ZL):
        for ref, which in ((own_ref, core), (other_ref, 1 - core)):
            at = pl.multiple_of((2 * zl + which) * block, block)
            piece = jnp.dot(
                act_ref[:, pl.ds(at, block)], ref[zl], preferred_element_type=jnp.float32
            )
            total = piece if total is None else total + piece
    out_ref[...] = total.astype(out_ref.dtype)


def on_device(activations, codes, scales, cotangent):
    width = activations.shape[1]
    head = cotangent.shape[1]
    tokens = activations.shape[0] * Y * ZH * X * ZL * CORE
    vmem = pl.BlockSpec(memory_space=pltpu.VMEM)
    smem = pl.BlockSpec(memory_space=pltpu.SMEM)
    params = pltpu.CompilerParams(vmem_limit_bytes=32 * 1024 * 1024)
    core = lax.axis_index("core").reshape(1).astype(jnp.int32)
    swap = [(0, 1), (1, 0)]

    stored = (codes.astype(jnp.float32) * scales[:, None, :]).astype(jnp.bfloat16)
    own = lax.all_gather(stored, "zl", axis=0, tiled=True)

    rows = width // CORE
    keep, send = pl.pallas_call(
        lambda *refs: term_kernel(float(tokens) ** (-0.5), *refs),
        out_shape=[jax.ShapeDtypeStruct((rows, head), jnp.float32)] * 2,
        in_specs=[smem, vmem, vmem],
        out_specs=[vmem, vmem],
        compiler_params=params,
        cost_estimate=pl.CostEstimate(flops=2 * 128 * width * head, bytes_accessed=3 << 20, transcendentals=0),
    )(core, activations, cotangent)
    chip = keep + lax.ppermute(send, "core", swap)
    got = lax.all_to_all(chip.astype(jnp.bfloat16), "x", 0, 0, tiled=True)
    line = got.reshape(X, rows // X, head).astype(jnp.float32).sum(0).astype(jnp.bfloat16)
    peers = Y * ZH * ZL
    got = lax.all_to_all(
        line.reshape(peers, rows // X // peers, head), ("y", "zh", "zl"), 0, 0, tiled=True
    )
    weight_grad = got.astype(jnp.float32).sum(0)

    other = lax.ppermute(own, "core", swap)
    values_out = pl.pallas_call(
        project_kernel,
        out_shape=jax.ShapeDtypeStruct(cotangent.shape, jnp.bfloat16),
        in_specs=[smem, vmem, vmem, vmem],
        out_specs=vmem,
        compiler_params=params,
        cost_estimate=pl.CostEstimate(flops=2 * 128 * width * head, bytes_accessed=2 << 20, transcendentals=0),
    )(core, activations, own, other)
    return values_out, weight_grad


def solution(mesh):
    fine = Mesh(mesh.devices.reshape(Y, ZH, X, ZL, CORE), AXES)
    tokens, local = P(AXES, None), ("zl", "core")
    return jax.shard_map(
        on_device,
        mesh=fine,
        in_specs=(tokens, P(local, None, None), P(local, None), tokens),
        out_specs=(tokens, tokens),
        check_vma=False,
    )
```

```python
import jax
import jax.numpy as jnp
from jax import lax
from jax.experimental import pallas as pl
from jax.experimental.pallas import tpu as pltpu
from jax.sharding import Mesh, PartitionSpec as P

Y, ZH, X, ZL, CORE = 8, 2, 4, 8, 2
AXES = ("y", "zh", "x", "zl", "core")


def term_kernel(scale, core_ref, act_ref, cot_ref, keep_ref, send_ref):
    first = core_ref[0] == 0
    share = 4
    per = act_ref.shape[1] // (Y * ZH)
    sub = per // X
    half = sub // 2
    cot = cot_ref[...]
    low = lax.broadcasted_iota(jnp.int32, (sub // 16, 8, cot.shape[1]), 1) < share
    for outer in range(Y * ZH):
        part = lax.dot_general(
            act_ref[:, outer * per : (outer + 1) * per],
            cot,
            (((0,), (0,)), ((), ())),
            preferred_element_type=jnp.float32,
        )
        part = part * scale
        for x in range(X):
            tiles = part[x * sub : (x + 1) * sub].reshape(sub // 16, 2, 8, cot.shape[1])
            even, odd = tiles[:, 0], tiles[:, 1]
            zero = jnp.where(low, even, pltpu.roll(odd, share, 1))
            one = jnp.where(low, pltpu.roll(even, share, 1), odd)
            at = pl.ds(((outer // ZH * X + x) * ZH + outer % ZH) * half, half)
            keep_ref[at, :] = jnp.where(first, zero, one).reshape(half, -1)
            send_ref[at, :] = jnp.where(first, one, zero).reshape(half, -1)


def project_kernel(place_ref, act_ref, own_ref, other_ref, out_ref):
    zl, core = place_ref[0], place_ref[1]
    sign = 1 - 2 * core
    block = own_ref.shape[0] // ZL
    total = None
    for step in range(ZL):
        at_rows = pl.ds(step * block, block)
        for ref, line, which in ((own_ref, zl + step * sign, core), (other_ref, zl - step * sign, 1 - core)):
            at = pl.multiple_of((2 * ((line + ZL) % ZL) + which) * block, block)
            piece = jnp.dot(
                act_ref[:, pl.ds(at, block)], ref[at_rows, :], preferred_element_type=jnp.float32
            )
            total = piece if total is None else total + piece
    out_ref[...] = total.astype(out_ref.dtype)


def along_z(value, shift):
    ring = ZH * ZL
    pairs = []
    for z in range(ring):
        pairs.append(((z + shift) % ring * CORE, z * CORE))
        pairs.append(((z - shift) % ring * CORE + 1, z * CORE + 1))
    return lax.ppermute(value, ("zh", "zl", "core"), pairs)


def on_device(activations, codes, scales, cotangent):
    width = activations.shape[1]
    head = cotangent.shape[1]
    tokens = activations.shape[0] * Y * ZH * X * ZL * CORE
    vmem = pl.BlockSpec(memory_space=pltpu.VMEM)
    smem = pl.BlockSpec(memory_space=pltpu.SMEM)
    params = pltpu.CompilerParams(vmem_limit_bytes=32 * 1024 * 1024)
    core = lax.axis_index("core").reshape(1).astype(jnp.int32)
    place = jnp.concatenate([lax.axis_index("zl").reshape(1).astype(jnp.int32), core])
    swap = [(0, 1), (1, 0)]

    stored = (codes.astype(jnp.float32) * scales[:, None, :]).astype(jnp.bfloat16)
    own = stored.reshape(-1, head)
    for shift in (1, 2, 4):
        own = jnp.concatenate([own, along_z(own, shift)])

    rows = width // CORE
    keep, send = pl.pallas_call(
        lambda *refs: term_kernel(float(tokens) ** (-0.5), *refs),
        out_shape=[jax.ShapeDtypeStruct((rows, head), jnp.float32)] * 2,
        in_specs=[smem, vmem, vmem],
        out_specs=[vmem, vmem],
        compiler_params=params,
        cost_estimate=pl.CostEstimate(flops=2 * 128 * width * head, bytes_accessed=3 << 20, transcendentals=0),
    )(core, activations, cotangent)
    chip = keep + lax.ppermute(send, "core", swap)
    got = lax.all_to_all(chip.astype(jnp.bfloat16), ("y", "x"), 0, 0, tiled=True)
    peers = ZH * ZL
    line = got.reshape(Y * X, peers, rows // (Y * X * peers), head).astype(jnp.float32).sum(0)
    weight_grad = lax.all_to_all(line, ("zh", "zl"), 0, 0, tiled=True).sum(0)

    other = lax.ppermute(own, "core", swap)
    values_out = pl.pallas_call(
        project_kernel,
        out_shape=jax.ShapeDtypeStruct(cotangent.shape, jnp.bfloat16),
        in_specs=[smem, vmem, vmem, vmem],
        out_specs=vmem,
        compiler_params=params,
        cost_estimate=pl.CostEstimate(flops=2 * 128 * width * head, bytes_accessed=2 << 20, transcendentals=0),
    )(place, activations, own, other)
    return values_out, weight_grad


def solution(mesh):
    fine = Mesh(mesh.devices.reshape(Y, ZH, X, ZL, CORE), AXES)
    tokens, local = P(AXES, None), ("zl", "core")
    return jax.shard_map(
        on_device,
        mesh=fine,
        in_specs=(tokens, P(local, None, None), P(local, None), tokens),
        out_specs=(tokens, tokens),
        check_vma=False,
    )
```

```python
import jax
import jax.numpy as jnp
from jax import lax
from jax.experimental import pallas as pl
from jax.experimental.pallas import tpu as pltpu
from jax.sharding import Mesh, PartitionSpec as P

Y, ZH, X, ZL, CORE = 8, 2, 4, 8, 2
AXES = ("y", "zh", "x", "zl", "core")
SHIFTS = (4, 2, 1)


def term_kernel(scale, core_ref, act_ref, cot_ref, keep_ref, send_ref):
    first = core_ref[0] == 0
    share = 4
    per = act_ref.shape[1] // (Y * ZH)
    sub = per // X
    half = sub // 2
    cot = cot_ref[...]
    low = lax.broadcasted_iota(jnp.int32, (sub // 16, 8, cot.shape[1]), 1) < share
    for outer in range(Y * ZH):
        part = lax.dot_general(
            act_ref[:, outer * per : (outer + 1) * per],
            cot,
            (((0,), (0,)), ((), ())),
            preferred_element_type=jnp.float32,
        )
        part = part * scale
        for x in range(X):
            tiles = part[x * sub : (x + 1) * sub].reshape(sub // 16, 2, 8, cot.shape[1])
            even, odd = tiles[:, 0], tiles[:, 1]
            zero = jnp.where(low, even, pltpu.roll(odd, share, 1))
            one = jnp.where(low, pltpu.roll(even, share, 1), odd)
            at = pl.ds(((outer // ZH * X + x) * ZH + outer % ZH) * half, half)
            keep_ref[at, :] = jnp.where(first, zero, one).reshape(half, -1)
            send_ref[at, :] = jnp.where(first, one, zero).reshape(half, -1)


def gather_order():
    held = [0]
    for shift in SHIFTS:
        held = held + [step + shift for step in held]
    return held


def project_kernel(place_ref, act_ref, own_ref, other_ref, out_ref):
    zl, core = place_ref[0], place_ref[1]
    sign = 1 - 2 * core
    block = own_ref.shape[0] // ZL
    total = None
    for place, step in enumerate(gather_order()):
        at_rows = pl.ds(place * block, block)
        for ref, line, which in ((own_ref, zl + step * sign, core), (other_ref, zl - step * sign, 1 - core)):
            at = pl.multiple_of((2 * ((line + ZL) % ZL) + which) * block, block)
            piece = jnp.dot(
                act_ref[:, pl.ds(at, block)], ref[at_rows, :], preferred_element_type=jnp.float32
            )
            total = piece if total is None else total + piece
    out_ref[...] = total.astype(out_ref.dtype)


def along_z(value, shift):
    ring = ZH * ZL
    pairs = []
    for z in range(ring):
        pairs.append(((z + shift) % ring * CORE, z * CORE))
        pairs.append(((z - shift) % ring * CORE + 1, z * CORE + 1))
    return lax.ppermute(value, ("zh", "zl", "core"), pairs)


def on_device(activations, codes, scales, cotangent):
    width = activations.shape[1]
    head = cotangent.shape[1]
    tokens = activations.shape[0] * Y * ZH * X * ZL * CORE
    vmem = pl.BlockSpec(memory_space=pltpu.VMEM)
    smem = pl.BlockSpec(memory_space=pltpu.SMEM)
    params = pltpu.CompilerParams(vmem_limit_bytes=32 * 1024 * 1024)
    core = lax.axis_index("core").reshape(1).astype(jnp.int32)
    place = jnp.concatenate([lax.axis_index("zl").reshape(1).astype(jnp.int32), core])
    swap = [(0, 1), (1, 0)]

    stored = (codes.astype(jnp.float32) * scales[:, None, :]).astype(jnp.bfloat16)
    own = stored.reshape(-1, head)
    for shift in SHIFTS:
        own = jnp.concatenate([own, along_z(own, shift)])

    rows = width // CORE
    keep, send = pl.pallas_call(
        lambda *refs: term_kernel(float(tokens) ** (-0.5), *refs),
        out_shape=[jax.ShapeDtypeStruct((rows, head), jnp.float32)] * 2,
        in_specs=[smem, vmem, vmem],
        out_specs=[vmem, vmem],
        compiler_params=params,
        cost_estimate=pl.CostEstimate(flops=2 * 128 * width * head, bytes_accessed=3 << 20, transcendentals=0),
    )(core, activations, cotangent)
    chip = keep + lax.ppermute(send, "core", swap)
    got = lax.all_to_all(chip.astype(jnp.bfloat16), ("y", "x"), 0, 0, tiled=True)
    peers = ZH * ZL
    line = got.reshape(Y * X, peers, rows // (Y * X * peers), head).astype(jnp.float32).sum(0)
    weight_grad = lax.all_to_all(line, ("zh", "zl"), 0, 0, tiled=True).sum(0)

    other = lax.ppermute(own, "core", swap)
    values_out = pl.pallas_call(
        project_kernel,
        out_shape=jax.ShapeDtypeStruct(cotangent.shape, jnp.bfloat16),
        in_specs=[smem, vmem, vmem, vmem],
        out_specs=vmem,
        compiler_params=params,
        cost_estimate=pl.CostEstimate(flops=2 * 128 * width * head, bytes_accessed=2 << 20, transcendentals=0),
    )(place, activations, own, other)
    return values_out, weight_grad


def solution(mesh):
    fine = Mesh(mesh.devices.reshape(Y, ZH, X, ZL, CORE), AXES)
    tokens, local = P(AXES, None), ("zl", "core")
    return jax.shard_map(
        on_device,
        mesh=fine,
        in_specs=(tokens, P(local, None, None), P(local, None), tokens),
        out_specs=(tokens, tokens),
        check_vma=False,
    )
```

```python
import jax
import jax.numpy as jnp
from jax import lax
from jax.experimental import pallas as pl
from jax.experimental.pallas import tpu as pltpu
from jax.sharding import Mesh, PartitionSpec as P

Y, ZH, X, ZL, CORE = 8, 2, 4, 8, 2
AXES = ("y", "zh", "x", "zl", "core")
FIRST, SECOND = 3, 1


def term_kernel(scale, core_ref, act_ref, cot_ref, keep_ref, send_ref):
    first = core_ref[0] == 0
    share = 4
    per = act_ref.shape[1] // (Y * ZH)
    sub = per // X
    half = sub // 2
    cot = cot_ref[...]
    low = lax.broadcasted_iota(jnp.int32, (sub // 16, 8, cot.shape[1]), 1) < share
    for outer in range(Y * ZH):
        part = lax.dot_general(
            act_ref[:, outer * per : (outer + 1) * per],
            cot,
            (((0,), (0,)), ((), ())),
            preferred_element_type=jnp.float32,
        )
        part = part * scale
        for x in range(X):
            tiles = part[x * sub : (x + 1) * sub].reshape(sub // 16, 2, 8, cot.shape[1])
            even, odd = tiles[:, 0], tiles[:, 1]
            zero = jnp.where(low, even, pltpu.roll(odd, share, 1))
            one = jnp.where(low, pltpu.roll(even, share, 1), odd)
            at = pl.ds(((outer // ZH * X + x) * ZH + outer % ZH) * half, half)
            keep_ref[at, :] = jnp.where(first, zero, one).reshape(half, -1)
            send_ref[at, :] = jnp.where(first, one, zero).reshape(half, -1)


def gather_order():
    held = [0, FIRST, -FIRST]
    return held + [step + SECOND for step in held] + [step - SECOND for step in held[:2]]


def project_kernel(place_ref, act_ref, own_ref, other_ref, out_ref):
    zl, core = place_ref[0], place_ref[1]
    steps = gather_order()
    block = own_ref.shape[0] // len(steps)
    total = None
    for place, step in enumerate(steps):
        line = 2 * ((zl + step + ZL) % ZL)
        rows = pl.ds(place * block, block)
        for ref, which in ((own_ref, core), (other_ref, 1 - core)):
            at = pl.multiple_of((line + which) * block, block)
            piece = jnp.dot(
                act_ref[:, pl.ds(at, block)], ref[rows, :], preferred_element_type=jnp.float32
            )
            total = piece if total is None else total + piece
    out_ref[...] = total.astype(out_ref.dtype)


def along_z(value, shift):
    ring = ZH * ZL
    pairs = [((z + shift) % ring, z) for z in range(ring)]
    return lax.ppermute(value, ("zh", "zl"), pairs)


def on_device(activations, codes, scales, cotangent):
    width = activations.shape[1]
    head = cotangent.shape[1]
    tokens = activations.shape[0] * Y * ZH * X * ZL * CORE
    vmem = pl.BlockSpec(memory_space=pltpu.VMEM)
    smem = pl.BlockSpec(memory_space=pltpu.SMEM)
    params = pltpu.CompilerParams(vmem_limit_bytes=32 * 1024 * 1024)
    core = lax.axis_index("core").reshape(1).astype(jnp.int32)
    place = jnp.concatenate([lax.axis_index("zl").reshape(1).astype(jnp.int32), core])
    swap = [(0, 1), (1, 0)]

    stored = (codes.astype(jnp.float32) * scales[:, None, :]).astype(jnp.bfloat16)
    own = stored.reshape(-1, head)

    rows = width // CORE
    keep, send = pl.pallas_call(
        lambda *refs: term_kernel(float(tokens) ** (-0.5), *refs),
        out_shape=[jax.ShapeDtypeStruct((rows, head), jnp.float32)] * 2,
        in_specs=[smem, vmem, vmem],
        out_specs=[vmem, vmem],
        compiler_params=params,
        cost_estimate=pl.CostEstimate(flops=2 * 128 * width * head, bytes_accessed=3 << 20, transcendentals=0),
    )(core, activations, cotangent)
    held = jnp.concatenate([own, along_z(own, FIRST), along_z(own, -FIRST)])
    chip = keep + lax.ppermute(send, "core", swap)
    chip = chip.astype(jnp.bfloat16)
    two = 2 * own.shape[0]
    own = jnp.concatenate([held, along_z(held, SECOND), along_z(held[:two], -SECOND)])
    got = lax.all_to_all(chip, ("y", "x"), 0, 0, tiled=True)
    peers = ZH * ZL
    line = got.reshape(Y * X, peers, rows // (Y * X * peers), head).astype(jnp.float32).sum(0)
    weight_grad = lax.all_to_all(line, ("zh", "zl"), 0, 0, tiled=True).sum(0)

    other = lax.ppermute(own, "core", swap)
    values_out = pl.pallas_call(
        project_kernel,
        out_shape=jax.ShapeDtypeStruct(cotangent.shape, jnp.bfloat16),
        in_specs=[smem, vmem, vmem, vmem],
        out_specs=vmem,
        compiler_params=params,
        cost_estimate=pl.CostEstimate(flops=2 * 128 * width * head, bytes_accessed=2 << 20, transcendentals=0),
    )(place, activations, own, other)
    return values_out, weight_grad


def solution(mesh):
    fine = Mesh(mesh.devices.reshape(Y, ZH, X, ZL, CORE), AXES)
    tokens, local = P(AXES, None), ("zl", "core")
    return jax.shard_map(
        on_device,
        mesh=fine,
        in_specs=(tokens, P(local, None, None), P(local, None), tokens),
        out_specs=(tokens, tokens),
        check_vma=False,
    )
```

```python
import jax
import jax.numpy as jnp
from jax import lax
from jax.experimental import pallas as pl
from jax.experimental.pallas import tpu as pltpu
from jax.sharding import Mesh, PartitionSpec as P

Y, ZH, X, ZL, CORE = 8, 2, 4, 8, 2
AXES = ("y", "zh", "x", "zl", "core")
FIRST, SECOND = 3, 1


def term_kernel(scale, core_ref, act_ref, cot_ref, keep_ref, send_ref):
    first = core_ref[0] == 0
    share = 4
    per = act_ref.shape[1] // (Y * ZH)
    sub = per // X
    half = sub // 2
    cot = cot_ref[...]
    low = lax.broadcasted_iota(jnp.int32, (sub // 16, 8, cot.shape[1]), 1) < share
    for outer in range(Y * ZH):
        part = lax.dot_general(
            act_ref[:, outer * per : (outer + 1) * per],
            cot,
            (((0,), (0,)), ((), ())),
            preferred_element_type=jnp.float32,
        )
        part = part * scale
        for x in range(X):
            tiles = part[x * sub : (x + 1) * sub].reshape(sub // 16, 2, 8, cot.shape[1])
            even, odd = tiles[:, 0], tiles[:, 1]
            zero = jnp.where(low, even, pltpu.roll(odd, share, 1))
            one = jnp.where(low, pltpu.roll(even, share, 1), odd)
            at = pl.ds(((outer // ZH * X + x) * ZH + outer % ZH) * half, half)
            keep_ref[at, :] = jnp.where(first, zero, one).reshape(half, -1)
            send_ref[at, :] = jnp.where(first, one, zero).reshape(half, -1)


def gather_order():
    held = [0, FIRST, -FIRST]
    return held + [step + SECOND for step in held] + [step - SECOND for step in held[:2]]


def project(place_ref, act_ref, shards_ref, which):
    zl = place_ref[0]
    steps = gather_order()
    block = shards_ref.shape[0] // len(steps)
    total = None
    for place, step in enumerate(steps):
        at = pl.multiple_of((2 * ((zl + step + ZL) % ZL) + which) * block, block)
        piece = jnp.dot(
            act_ref[:, pl.ds(at, block)],
            shards_ref[pl.ds(place * block, block), :],
            preferred_element_type=jnp.float32,
        )
        total = piece if total is None else total + piece
    return total


def own_kernel(place_ref, act_ref, own_ref, out_ref):
    out_ref[...] = project(place_ref, act_ref, own_ref, place_ref[1])


def other_kernel(place_ref, act_ref, other_ref, part_ref, out_ref):
    total = part_ref[...] + project(place_ref, act_ref, other_ref, 1 - place_ref[1])
    out_ref[...] = total.astype(out_ref.dtype)


def along_z(value, shift):
    ring = ZH * ZL
    pairs = [((z + shift) % ring, z) for z in range(ring)]
    return lax.ppermute(value, ("zh", "zl"), pairs)


def on_device(activations, codes, scales, cotangent):
    width = activations.shape[1]
    head = cotangent.shape[1]
    tokens = activations.shape[0] * Y * ZH * X * ZL * CORE
    vmem = pl.BlockSpec(memory_space=pltpu.VMEM)
    smem = pl.BlockSpec(memory_space=pltpu.SMEM)
    params = pltpu.CompilerParams(vmem_limit_bytes=32 * 1024 * 1024)
    core = lax.axis_index("core").reshape(1).astype(jnp.int32)
    place = jnp.concatenate([lax.axis_index("zl").reshape(1).astype(jnp.int32), core])
    swap = [(0, 1), (1, 0)]

    stored = (codes.astype(jnp.float32) * scales[:, None, :]).astype(jnp.bfloat16)
    own = stored.reshape(-1, head)

    rows = width // CORE
    keep, send = pl.pallas_call(
        lambda *refs: term_kernel(float(tokens) ** (-0.5), *refs),
        out_shape=[jax.ShapeDtypeStruct((rows, head), jnp.float32)] * 2,
        in_specs=[smem, vmem, vmem],
        out_specs=[vmem, vmem],
        compiler_params=params,
        cost_estimate=pl.CostEstimate(flops=2 * 128 * width * head, bytes_accessed=3 << 20, transcendentals=0),
    )(core, activations, cotangent)
    held = jnp.concatenate([own, along_z(own, FIRST), along_z(own, -FIRST)])
    keep, _ = lax.optimization_barrier((keep, own))
    chip = keep + lax.ppermute(send, "core", swap)
    chip = chip.astype(jnp.bfloat16)
    ahead, back = along_z(held, SECOND), along_z(held[: 2 * own.shape[0]], -SECOND)
    got = lax.all_to_all(chip, ("y", "x"), 0, 0, tiled=True)
    peers = ZH * ZL
    line = got.reshape(Y * X, peers, rows // (Y * X * peers), head).astype(jnp.float32).sum(0)
    ahead, back, _ = lax.optimization_barrier((ahead, back, line))
    own = jnp.concatenate([held, ahead, back])
    weight_grad = lax.all_to_all(line, ("zh", "zl"), 0, 0, tiled=True).sum(0)

    part = pl.pallas_call(
        own_kernel,
        out_shape=jax.ShapeDtypeStruct(cotangent.shape, jnp.float32),
        in_specs=[smem, vmem, vmem],
        out_specs=vmem,
        compiler_params=params,
        cost_estimate=pl.CostEstimate(flops=10**11, bytes_accessed=1 << 20, transcendentals=0),
    )(place, activations, own)
    other = lax.ppermute(own, "core", swap)
    values_out = pl.pallas_call(
        other_kernel,
        out_shape=jax.ShapeDtypeStruct(cotangent.shape, jnp.bfloat16),
        in_specs=[smem, vmem, vmem, vmem],
        out_specs=vmem,
        compiler_params=params,
        cost_estimate=pl.CostEstimate(flops=128 * width * head, bytes_accessed=1 << 20, transcendentals=0),
    )(place, activations, other, part)
    return values_out, weight_grad


def solution(mesh):
    fine = Mesh(mesh.devices.reshape(Y, ZH, X, ZL, CORE), AXES)
    tokens, local = P(AXES, None), ("zl", "core")
    return jax.shard_map(
        on_device,
        mesh=fine,
        in_specs=(tokens, P(local, None, None), P(local, None), tokens),
        out_specs=(tokens, tokens),
        check_vma=False,
    )
```

```python
import jax
import jax.numpy as jnp
from jax import lax
from jax.experimental import pallas as pl
from jax.experimental.pallas import tpu as pltpu
from jax.sharding import Mesh, PartitionSpec as P

Y, ZH, X, ZL, CORE = 8, 2, 4, 8, 2
AXES = ("y", "zh", "x", "zl", "core")
FIRST, SECOND = 3, 1


def term_kernel(scale, core_ref, act_ref, cot_ref, keep_ref, send_ref):
    first = core_ref[0] == 0
    share = 4
    per = act_ref.shape[1] // (Y * ZH)
    sub = per // X
    half = sub // 2
    cot = cot_ref[...]
    low = lax.broadcasted_iota(jnp.int32, (sub // 16, 8, cot.shape[1]), 1) < share
    for outer in range(Y * ZH):
        part = lax.dot_general(
            act_ref[:, outer * per : (outer + 1) * per],
            cot,
            (((0,), (0,)), ((), ())),
            preferred_element_type=jnp.float32,
        )
        part = part * scale
        for x in range(X):
            tiles = part[x * sub : (x + 1) * sub].reshape(sub // 16, 2, 8, cot.shape[1])
            even, odd = tiles[:, 0], tiles[:, 1]
            zero = jnp.where(low, even, pltpu.roll(odd, share, 1))
            one = jnp.where(low, pltpu.roll(even, share, 1), odd)
            at = pl.ds((x * Y * ZH + outer) * half, half)
            keep_ref[at, :] = jnp.where(first, zero, one).reshape(half, -1)
            send_ref[at, :] = jnp.where(first, one, zero).reshape(half, -1)


def gather_order():
    held = [0, FIRST, -FIRST]
    return held + [step + SECOND for step in held] + [step - SECOND for step in held[:2]]


def project(place_ref, act_ref, shards_ref, which):
    zl = place_ref[0]
    steps = gather_order()
    block = shards_ref.shape[0] // len(steps)
    total = None
    for place, step in enumerate(steps):
        at = pl.multiple_of((2 * ((zl + step + ZL) % ZL) + which) * block, block)
        piece = jnp.dot(
            act_ref[:, pl.ds(at, block)],
            shards_ref[pl.ds(place * block, block), :],
            preferred_element_type=jnp.float32,
        )
        total = piece if total is None else total + piece
    return total


def own_kernel(place_ref, act_ref, own_ref, out_ref):
    out_ref[...] = project(place_ref, act_ref, own_ref, place_ref[1])


def other_kernel(place_ref, act_ref, other_ref, part_ref, out_ref):
    total = part_ref[...] + project(place_ref, act_ref, other_ref, 1 - place_ref[1])
    out_ref[...] = total.astype(out_ref.dtype)


def along_z(value, shift):
    ring = ZH * ZL
    pairs = [((z + shift) % ring, z) for z in range(ring)]
    return lax.ppermute(value, ("zh", "zl"), pairs)


def on_device(activations, codes, scales, cotangent):
    width = activations.shape[1]
    head = cotangent.shape[1]
    tokens = activations.shape[0] * Y * ZH * X * ZL * CORE
    vmem = pl.BlockSpec(memory_space=pltpu.VMEM)
    smem = pl.BlockSpec(memory_space=pltpu.SMEM)
    params = pltpu.CompilerParams(vmem_limit_bytes=32 * 1024 * 1024)
    core = lax.axis_index("core").reshape(1).astype(jnp.int32)
    place = jnp.concatenate([lax.axis_index("zl").reshape(1).astype(jnp.int32), core])
    swap = [(0, 1), (1, 0)]

    stored = (codes.astype(jnp.float32) * scales[:, None, :]).astype(jnp.bfloat16)
    own = stored.reshape(-1, head)

    rows = width // CORE
    keep, send = pl.pallas_call(
        lambda *refs: term_kernel(float(tokens) ** (-0.5), *refs),
        out_shape=[jax.ShapeDtypeStruct((rows, head), jnp.float32)] * 2,
        in_specs=[smem, vmem, vmem],
        out_specs=[vmem, vmem],
        compiler_params=params,
        cost_estimate=pl.CostEstimate(flops=2 * 128 * width * head, bytes_accessed=3 << 20, transcendentals=0),
    )(core, activations, cotangent)
    far = along_z(own, FIRST), along_z(own, -FIRST)
    keep, _ = lax.optimization_barrier((keep, own))
    chip = (keep + lax.ppermute(send, "core", swap)).astype(jnp.bfloat16)
    got = lax.all_to_all(chip, "x", 0, 0, tiled=True)
    line = got.reshape(X, rows // X, head).astype(jnp.float32).sum(0).astype(jnp.bfloat16)
    *far, _ = lax.optimization_barrier((*far, line))
    held = jnp.concatenate([own, *far])
    ahead, back = along_z(held, SECOND), along_z(held[: 2 * own.shape[0]], -SECOND)
    got = lax.all_to_all(line, "y", 0, 0, tiled=True)
    peers = ZH * ZL
    line = got.reshape(Y, peers, rows // (X * Y * peers), head).astype(jnp.float32).sum(0)
    ahead, back, _ = lax.optimization_barrier((ahead, back, line))
    own = jnp.concatenate([held, ahead, back])
    weight_grad = lax.all_to_all(line, ("zh", "zl"), 0, 0, tiled=True).sum(0)

    part = pl.pallas_call(
        own_kernel,
        out_shape=jax.ShapeDtypeStruct(cotangent.shape, jnp.float32),
        in_specs=[smem, vmem, vmem],
        out_specs=vmem,
        compiler_params=params,
        cost_estimate=pl.CostEstimate(flops=10**11, bytes_accessed=1 << 20, transcendentals=0),
    )(place, activations, own)
    other = lax.ppermute(own, "core", swap)
    values_out = pl.pallas_call(
        other_kernel,
        out_shape=jax.ShapeDtypeStruct(cotangent.shape, jnp.bfloat16),
        in_specs=[smem, vmem, vmem, vmem],
        out_specs=vmem,
        compiler_params=params,
        cost_estimate=pl.CostEstimate(flops=128 * width * head, bytes_accessed=1 << 20, transcendentals=0),
    )(place, activations, other, part)
    return values_out, weight_grad


def solution(mesh):
    fine = Mesh(mesh.devices.reshape(Y, ZH, X, ZL, CORE), AXES)
    tokens, local = P(AXES, None), ("zl", "core")
    return jax.shard_map(
        on_device,
        mesh=fine,
        in_specs=(tokens, P(local, None, None), P(local, None), tokens),
        out_specs=(tokens, tokens),
        check_vma=False,
    )
```

```python
import jax
import jax.numpy as jnp
from jax import lax
from jax.experimental import pallas as pl
from jax.experimental.pallas import tpu as pltpu
from jax.sharding import Mesh, PartitionSpec as P

Y, ZH, X, ZL, CORE = 8, 2, 4, 8, 2
AXES = ("y", "zh", "x", "zl", "core")
FIRST, SECOND = 3, 1


def term_kernel(scale, core_ref, act_ref, cot_ref, keep_ref, send_ref):
    first = core_ref[0] == 0
    share = 4
    per = act_ref.shape[1] // (Y * ZH)
    sub = per // X
    half = sub // 2
    cot = cot_ref[...]
    low = lax.broadcasted_iota(jnp.int32, (sub // 16, 8, cot.shape[1]), 1) < share
    for outer in range(Y * ZH):
        part = lax.dot_general(
            act_ref[:, outer * per : (outer + 1) * per],
            cot,
            (((0,), (0,)), ((), ())),
            preferred_element_type=jnp.float32,
        )
        part = part * scale
        for x in range(X):
            tiles = part[x * sub : (x + 1) * sub].reshape(sub // 16, 2, 8, cot.shape[1])
            even, odd = tiles[:, 0], tiles[:, 1]
            zero = jnp.where(low, even, pltpu.roll(odd, share, 1))
            one = jnp.where(low, pltpu.roll(even, share, 1), odd)
            at = pl.ds(((outer // ZH * X + x) * ZH + outer % ZH) * half, half)
            keep_ref[at, :] = jnp.where(first, zero, one).reshape(half, -1)
            send_ref[at, :] = jnp.where(first, one, zero).reshape(half, -1).astype(send_ref.dtype)


def gather_order():
    held = [0, FIRST, -FIRST]
    return held + [step + SECOND for step in held] + [step - SECOND for step in held[:2]]


def project_kernel(place_ref, act_ref, own_ref, other_ref, out_ref):
    zl, core = place_ref[0], place_ref[1]
    steps = gather_order()
    block = own_ref.shape[0] // len(steps)
    total = None
    for place, step in enumerate(steps):
        line = 2 * ((zl + step + ZL) % ZL)
        rows = pl.ds(place * block, block)
        for ref, which in ((own_ref, core), (other_ref, 1 - core)):
            at = pl.multiple_of((line + which) * block, block)
            piece = jnp.dot(
                act_ref[:, pl.ds(at, block)], ref[rows, :], preferred_element_type=jnp.float32
            )
            total = piece if total is None else total + piece
    out_ref[...] = total.astype(out_ref.dtype)


def along_z(value, shift):
    ring = ZH * ZL
    pairs = [((z + shift) % ring, z) for z in range(ring)]
    return lax.ppermute(value, ("zh", "zl"), pairs)


def on_device(activations, codes, scales, cotangent):
    width = activations.shape[1]
    head = cotangent.shape[1]
    tokens = activations.shape[0] * Y * ZH * X * ZL * CORE
    vmem = pl.BlockSpec(memory_space=pltpu.VMEM)
    smem = pl.BlockSpec(memory_space=pltpu.SMEM)
    params = pltpu.CompilerParams(vmem_limit_bytes=32 * 1024 * 1024)
    core = lax.axis_index("core").reshape(1).astype(jnp.int32)
    place = jnp.concatenate([lax.axis_index("zl").reshape(1).astype(jnp.int32), core])
    swap = [(0, 1), (1, 0)]

    stored = (codes.astype(jnp.float32) * scales[:, None, :]).astype(jnp.bfloat16)
    own = stored.reshape(-1, head)

    rows = width // CORE
    keep, send = pl.pallas_call(
        lambda *refs: term_kernel(float(tokens) ** (-0.5), *refs),
        out_shape=[
            jax.ShapeDtypeStruct((rows, head), jnp.float32),
            jax.ShapeDtypeStruct((rows, head), jnp.bfloat16),
        ],
        in_specs=[smem, vmem, vmem],
        out_specs=[vmem, vmem],
        compiler_params=params,
        cost_estimate=pl.CostEstimate(flops=2 * 128 * width * head, bytes_accessed=3 << 20, transcendentals=0),
    )(core, activations, cotangent)
    held = jnp.concatenate([own, along_z(own, FIRST), along_z(own, -FIRST)])
    chip = keep + lax.ppermute(send, "core", swap).astype(jnp.float32)
    chip = chip.astype(jnp.bfloat16)
    two = 2 * own.shape[0]
    own = jnp.concatenate([held, along_z(held, SECOND), along_z(held[:two], -SECOND)])
    got = lax.all_to_all(chip, ("y", "x"), 0, 0, tiled=True)
    peers = ZH * ZL
    line = got.reshape(Y * X, peers, rows // (Y * X * peers), head).astype(jnp.float32).sum(0)
    weight_grad = lax.all_to_all(line, ("zh", "zl"), 0, 0, tiled=True).sum(0)

    other = lax.ppermute(own, "core", swap)
    values_out = pl.pallas_call(
        project_kernel,
        out_shape=jax.ShapeDtypeStruct(cotangent.shape, jnp.bfloat16),
        in_specs=[smem, vmem, vmem, vmem],
        out_specs=vmem,
        compiler_params=params,
        cost_estimate=pl.CostEstimate(flops=2 * 128 * width * head, bytes_accessed=2 << 20, transcendentals=0),
    )(place, activations, own, other)
    return values_out, weight_grad


def solution(mesh):
    fine = Mesh(mesh.devices.reshape(Y, ZH, X, ZL, CORE), AXES)
    tokens, local = P(AXES, None), ("zl", "core")
    return jax.shard_map(
        on_device,
        mesh=fine,
        in_specs=(tokens, P(local, None, None), P(local, None), tokens),
        out_specs=(tokens, tokens),
        check_vma=False,
    )
```

```python
import jax
import jax.numpy as jnp
from jax import lax
from jax.experimental import pallas as pl
from jax.experimental.pallas import tpu as pltpu
from jax.sharding import Mesh, PartitionSpec as P

Y, ZH, X, ZL, CORE = 8, 2, 4, 8, 2
AXES = ("y", "zh", "x", "zl", "core")
CHUNKS = 4
FIRST, SECOND = 3, 1


def term_kernel(scale, core_ref, act_hbm, cot_hbm, keep_ref, send_ref, act_ref, cot_ref, sems):
    first = core_ref[0] == 0
    share = 4
    per = act_ref.shape[1] // (Y * ZH)
    sub = per // X
    half = sub // 2
    wide = act_ref.shape[1] // CHUNKS
    copies = [pltpu.make_async_copy(cot_hbm, cot_ref, sems.at[CHUNKS])]
    for chunk in range(CHUNKS):
        at = pl.ds(chunk * wide, wide)
        copies.append(pltpu.make_async_copy(act_hbm.at[:, at], act_ref.at[:, at], sems.at[chunk]))
    for copy in copies:
        copy.start()
    copies[0].wait()
    cot = cot_ref[...]
    low = lax.broadcasted_iota(jnp.int32, (sub // 16, 8, cot.shape[1]), 1) < share
    for outer in range(Y * ZH):
        if outer * per % wide == 0:
            copies[1 + outer * per // wide].wait()
        part = lax.dot_general(
            act_ref[:, outer * per : (outer + 1) * per],
            cot,
            (((0,), (0,)), ((), ())),
            preferred_element_type=jnp.float32,
        )
        part = part * scale
        for x in range(X):
            tiles = part[x * sub : (x + 1) * sub].reshape(sub // 16, 2, 8, cot.shape[1])
            even, odd = tiles[:, 0], tiles[:, 1]
            zero = jnp.where(low, even, pltpu.roll(odd, share, 1))
            one = jnp.where(low, pltpu.roll(even, share, 1), odd)
            at = pl.ds(((outer // ZH * X + x) * ZH + outer % ZH) * half, half)
            keep_ref[at, :] = jnp.where(first, zero, one).reshape(half, -1)
            send_ref[at, :] = jnp.where(first, one, zero).reshape(half, -1)


def gather_order():
    held = [0, FIRST, -FIRST]
    return held + [step + SECOND for step in held] + [step - SECOND for step in held[:2]]


def project(place_ref, act_ref, shards_ref, which):
    zl = place_ref[0]
    steps = gather_order()
    block = shards_ref.shape[0] // len(steps)
    total = None
    for place, step in enumerate(steps):
        at = pl.multiple_of((2 * ((zl + step + ZL) % ZL) + which) * block, block)
        piece = jnp.dot(
            act_ref[:, pl.ds(at, block)],
            shards_ref[pl.ds(place * block, block), :],
            preferred_element_type=jnp.float32,
        )
        total = piece if total is None else total + piece
    return total


def own_kernel(place_ref, act_ref, own_ref, out_ref):
    out_ref[...] = project(place_ref, act_ref, own_ref, place_ref[1])


def other_kernel(place_ref, act_ref, other_ref, part_ref, out_ref):
    total = part_ref[...] + project(place_ref, act_ref, other_ref, 1 - place_ref[1])
    out_ref[...] = total.astype(out_ref.dtype)


def along_z(value, shift):
    ring = ZH * ZL
    pairs = [((z + shift) % ring, z) for z in range(ring)]
    return lax.ppermute(value, ("zh", "zl"), pairs)


def on_device(activations, codes, scales, cotangent):
    width = activations.shape[1]
    head = cotangent.shape[1]
    tokens = activations.shape[0] * Y * ZH * X * ZL * CORE
    vmem = pl.BlockSpec(memory_space=pltpu.VMEM)
    smem = pl.BlockSpec(memory_space=pltpu.SMEM)
    hbm = pl.BlockSpec(memory_space=pltpu.HBM)
    params = pltpu.CompilerParams(vmem_limit_bytes=32 * 1024 * 1024)
    core = lax.axis_index("core").reshape(1).astype(jnp.int32)
    place = jnp.concatenate([lax.axis_index("zl").reshape(1).astype(jnp.int32), core])
    swap = [(0, 1), (1, 0)]

    stored = (codes.astype(jnp.float32) * scales[:, None, :]).astype(jnp.bfloat16)
    own = stored.reshape(-1, head)

    rows = width // CORE
    keep, send = pl.pallas_call(
        lambda *refs: term_kernel(float(tokens) ** (-0.5), *refs),
        out_shape=[jax.ShapeDtypeStruct((rows, head), jnp.float32)] * 2,
        in_specs=[smem, hbm, hbm],
        out_specs=[vmem, vmem],
        scratch_shapes=[
            pltpu.VMEM(activations.shape, activations.dtype),
            pltpu.VMEM(cotangent.shape, cotangent.dtype),
            pltpu.SemaphoreType.DMA((CHUNKS + 1,)),
        ],
        compiler_params=pltpu.CompilerParams(vmem_limit_bytes=56 * 1024 * 1024),
        cost_estimate=pl.CostEstimate(flops=2 * 128 * width * head, bytes_accessed=3 << 20, transcendentals=0),
    )(core, activations, cotangent)
    held = jnp.concatenate([own, along_z(own, FIRST), along_z(own, -FIRST)])
    chip = keep + lax.ppermute(send, "core", swap)
    chip = chip.astype(jnp.bfloat16)
    two = 2 * own.shape[0]
    own = jnp.concatenate([held, along_z(held, SECOND), along_z(held[:two], -SECOND)])
    got = lax.all_to_all(chip, ("y", "x"), 0, 0, tiled=True)
    peers = ZH * ZL
    line = got.reshape(Y * X, peers, rows // (Y * X * peers), head).astype(jnp.float32).sum(0)
    weight_grad = lax.all_to_all(line, ("zh", "zl"), 0, 0, tiled=True).sum(0)

    part = pl.pallas_call(
        own_kernel,
        out_shape=jax.ShapeDtypeStruct(cotangent.shape, jnp.float32),
        in_specs=[smem, vmem, vmem],
        out_specs=vmem,
        compiler_params=params,
        cost_estimate=pl.CostEstimate(flops=128 * width * head, bytes_accessed=1 << 20, transcendentals=0),
    )(place, activations, own)
    other = lax.ppermute(own, "core", swap)
    values_out = pl.pallas_call(
        other_kernel,
        out_shape=jax.ShapeDtypeStruct(cotangent.shape, jnp.bfloat16),
        in_specs=[smem, vmem, vmem, vmem],
        out_specs=vmem,
        compiler_params=params,
        cost_estimate=pl.CostEstimate(flops=128 * width * head, bytes_accessed=1 << 20, transcendentals=0),
    )(place, activations, other, part)
    return values_out, weight_grad


def solution(mesh):
    fine = Mesh(mesh.devices.reshape(Y, ZH, X, ZL, CORE), AXES)
    tokens, local = P(AXES, None), ("zl", "core")
    return jax.shard_map(
        on_device,
        mesh=fine,
        in_specs=(tokens, P(local, None, None), P(local, None), tokens),
        out_specs=(tokens, tokens),
        check_vma=False,
    )
```

```python
import jax
import jax.numpy as jnp
from jax import lax
from jax.experimental import pallas as pl
from jax.experimental.pallas import tpu as pltpu
from jax.sharding import Mesh, PartitionSpec as P

Y, ZH, X, ZL, CORE = 8, 2, 4, 8, 2
AXES = ("y", "zh", "x", "zl", "core")
FIRST, SECOND = 3, 1


def term_kernel(scale, core_ref, act_ref, cot_ref, keep_ref, send_ref):
    first = core_ref[0] == 0
    share = 4
    per = act_ref.shape[1] // (Y * ZH)
    sub = per // X
    half = sub // 2
    cot = cot_ref[...]
    low = lax.broadcasted_iota(jnp.int32, (sub // 16, 8, cot.shape[1]), 1) < share
    for outer in range(Y * ZH):
        part = lax.dot_general(
            act_ref[:, outer * per : (outer + 1) * per],
            cot,
            (((0,), (0,)), ((), ())),
            preferred_element_type=jnp.float32,
        )
        part = part * scale
        for x in range(X):
            tiles = part[x * sub : (x + 1) * sub].reshape(sub // 16, 2, 8, cot.shape[1])
            even, odd = tiles[:, 0], tiles[:, 1]
            zero = jnp.where(low, even, pltpu.roll(odd, share, 1))
            one = jnp.where(low, pltpu.roll(even, share, 1), odd)
            at = pl.ds(((outer // ZH * X + x) * ZH + outer % ZH) * half, half)
            keep_ref[at, :] = jnp.where(first, zero, one).reshape(half, -1)
            send_ref[at, :] = jnp.where(first, one, zero).reshape(half, -1)


def gather_order():
    held = [0, FIRST, -FIRST]
    return held + [step + SECOND for step in held] + [step - SECOND for step in held[:2]]


def project(place_ref, act_ref, shards_ref, which):
    zl = place_ref[0]
    steps = gather_order()
    block = shards_ref.shape[0] // len(steps)
    total = None
    for place, step in enumerate(steps):
        at = pl.multiple_of((2 * ((zl + step + ZL) % ZL) + which) * block, block)
        piece = jnp.dot(
            act_ref[:, pl.ds(at, block)],
            shards_ref[pl.ds(place * block, block), :],
            preferred_element_type=jnp.float32,
        )
        total = piece if total is None else total + piece
    return total


def own_kernel(place_ref, act_ref, own_ref, out_ref):
    out_ref[...] = project(place_ref, act_ref, own_ref, place_ref[1])


def other_kernel(place_ref, act_ref, other_ref, part_ref, out_ref):
    total = part_ref[...] + project(place_ref, act_ref, other_ref, 1 - place_ref[1])
    out_ref[...] = total.astype(out_ref.dtype)


def along_z(value, shift):
    ring = ZH * ZL
    pairs = [((z + shift) % ring, z) for z in range(ring)]
    return lax.ppermute(value, ("zh", "zl"), pairs)


def on_device(activations, codes, scales, cotangent):
    width = activations.shape[1]
    head = cotangent.shape[1]
    tokens = activations.shape[0] * Y * ZH * X * ZL * CORE
    vmem = pl.BlockSpec(memory_space=pltpu.VMEM)
    smem = pl.BlockSpec(memory_space=pltpu.SMEM)
    params = pltpu.CompilerParams(vmem_limit_bytes=32 * 1024 * 1024)
    core = lax.axis_index("core").reshape(1).astype(jnp.int32)
    place = jnp.concatenate([lax.axis_index("zl").reshape(1).astype(jnp.int32), core])
    swap = [(0, 1), (1, 0)]

    stored = (codes.astype(jnp.float32) * scales[:, None, :]).astype(jnp.bfloat16)
    own = stored.reshape(-1, head)

    rows = width // CORE
    keep, send = pl.pallas_call(
        lambda *refs: term_kernel(float(tokens) ** (-0.5), *refs),
        out_shape=[jax.ShapeDtypeStruct((rows, head), jnp.float32)] * 2,
        in_specs=[smem, vmem, vmem],
        out_specs=[vmem, vmem],
        compiler_params=params,
        cost_estimate=pl.CostEstimate(flops=2 * 128 * width * head, bytes_accessed=3 << 20, transcendentals=0),
    )(core, activations, cotangent)
    held = jnp.concatenate([own, along_z(own, FIRST), along_z(own, -FIRST)])
    chip = keep + lax.ppermute(send, "core", swap)
    chip = chip.astype(jnp.bfloat16)
    two = 2 * own.shape[0]
    own = jnp.concatenate([held, along_z(held, SECOND), along_z(held[:two], -SECOND)])
    got = lax.all_to_all(chip, ("y", "x"), 0, 0, tiled=True)
    peers = ZH * ZL
    line = got.reshape(Y * X, peers, rows // (Y * X * peers), head).astype(jnp.float32).sum(0)
    weight_grad = lax.all_to_all(line, ("zh", "zl"), 0, 0, tiled=True).sum(0)

    part = pl.pallas_call(
        own_kernel,
        out_shape=jax.ShapeDtypeStruct(cotangent.shape, jnp.float32),
        in_specs=[smem, vmem, vmem],
        out_specs=vmem,
        compiler_params=params,
        cost_estimate=pl.CostEstimate(flops=128 * width * head, bytes_accessed=1 << 20, transcendentals=0),
    )(place, activations, own)
    other = lax.ppermute(own, "core", swap)
    values_out = pl.pallas_call(
        other_kernel,
        out_shape=jax.ShapeDtypeStruct(cotangent.shape, jnp.bfloat16),
        in_specs=[smem, vmem, vmem, vmem],
        out_specs=vmem,
        compiler_params=params,
        cost_estimate=pl.CostEstimate(flops=128 * width * head, bytes_accessed=1 << 20, transcendentals=0),
    )(place, activations, other, part)
    return values_out, weight_grad


def solution(mesh):
    fine = Mesh(mesh.devices.reshape(Y, ZH, X, ZL, CORE), AXES)
    tokens, local = P(AXES, None), ("zl", "core")
    return jax.shard_map(
        on_device,
        mesh=fine,
        in_specs=(tokens, P(local, None, None), P(local, None), tokens),
        out_specs=(tokens, tokens),
        check_vma=False,
    )
```

```python
import jax
import jax.numpy as jnp
from jax import lax
from jax.experimental import pallas as pl
from jax.experimental.pallas import tpu as pltpu
from jax.sharding import Mesh, PartitionSpec as P

Y, ZH, X, ZL, CORE = 8, 2, 4, 8, 2
AXES = ("y", "zh", "x", "zl", "core")
FIRST, SECOND = 3, 1


def term_kernel(scale, core_ref, act_ref, cot_ref, keep_ref, send_ref):
    first = core_ref[0] == 0
    share = 4
    per = act_ref.shape[1] // (Y * ZH)
    sub = per // X
    half = sub // 2
    cot = cot_ref[...]
    low = lax.broadcasted_iota(jnp.int32, (sub // 16, 8, cot.shape[1]), 1) < share
    for outer in range(Y * ZH):
        part = lax.dot_general(
            act_ref[:, outer * per : (outer + 1) * per],
            cot,
            (((0,), (0,)), ((), ())),
            preferred_element_type=jnp.float32,
        )
        part = part * scale
        for x in range(X):
            tiles = part[x * sub : (x + 1) * sub].reshape(sub // 16, 2, 8, cot.shape[1])
            even, odd = tiles[:, 0], tiles[:, 1]
            zero = jnp.where(low, even, pltpu.roll(odd, share, 1))
            one = jnp.where(low, pltpu.roll(even, share, 1), odd)
            at = pl.ds((x * Y * ZH + outer) * half, half)
            keep_ref[at, :] = jnp.where(first, zero, one).reshape(half, -1)
            send_ref[at, :] = jnp.where(first, one, zero).reshape(half, -1)


def gather_order():
    held = [0, FIRST, -FIRST]
    return held + [step + SECOND for step in held] + [step - SECOND for step in held[:2]]


def project_kernel(place_ref, act_ref, own_ref, other_ref, out_ref):
    zl, core = place_ref[0], place_ref[1]
    steps = gather_order()
    block = own_ref.shape[0] // len(steps)
    total = None
    for place, step in enumerate(steps):
        line = 2 * ((zl + step + ZL) % ZL)
        rows = pl.ds(place * block, block)
        for ref, which in ((own_ref, core), (other_ref, 1 - core)):
            at = pl.multiple_of((line + which) * block, block)
            piece = jnp.dot(
                act_ref[:, pl.ds(at, block)], ref[rows, :], preferred_element_type=jnp.float32
            )
            total = piece if total is None else total + piece
    out_ref[...] = total.astype(out_ref.dtype)


def along_z(value, shift):
    ring = ZH * ZL
    pairs = [((z + shift) % ring, z) for z in range(ring)]
    return lax.ppermute(value, ("zh", "zl"), pairs)


def on_device(activations, codes, scales, cotangent):
    width = activations.shape[1]
    head = cotangent.shape[1]
    tokens = activations.shape[0] * Y * ZH * X * ZL * CORE
    vmem = pl.BlockSpec(memory_space=pltpu.VMEM)
    smem = pl.BlockSpec(memory_space=pltpu.SMEM)
    params = pltpu.CompilerParams(vmem_limit_bytes=32 * 1024 * 1024)
    core = lax.axis_index("core").reshape(1).astype(jnp.int32)
    place = jnp.concatenate([lax.axis_index("zl").reshape(1).astype(jnp.int32), core])
    swap = [(0, 1), (1, 0)]

    stored = (codes.astype(jnp.float32) * scales[:, None, :]).astype(jnp.bfloat16)
    own = stored.reshape(-1, head)

    rows = width // CORE
    keep, send = pl.pallas_call(
        lambda *refs: term_kernel(float(tokens) ** (-0.5), *refs),
        out_shape=[jax.ShapeDtypeStruct((rows, head), jnp.float32)] * 2,
        in_specs=[smem, vmem, vmem],
        out_specs=[vmem, vmem],
        compiler_params=params,
        cost_estimate=pl.CostEstimate(flops=2 * 128 * width * head, bytes_accessed=3 << 20, transcendentals=0),
    )(core, activations, cotangent)
    held = jnp.concatenate([own, along_z(own, FIRST), along_z(own, -FIRST)])
    chip = keep + lax.ppermute(send, "core", swap)
    chip = chip.astype(jnp.bfloat16)
    two = 2 * own.shape[0]
    own = jnp.concatenate([held, along_z(held, SECOND), along_z(held[:two], -SECOND)])
    got = lax.all_to_all(chip, ("x", "y"), 0, 0, tiled=True)
    peers = ZH * ZL
    line = got.reshape(Y * X, peers, rows // (Y * X * peers), head).astype(jnp.float32).sum(0)
    weight_grad = lax.all_to_all(line, ("zh", "zl"), 0, 0, tiled=True).sum(0)

    other = lax.ppermute(own, "core", swap)
    values_out = pl.pallas_call(
        project_kernel,
        out_shape=jax.ShapeDtypeStruct(cotangent.shape, jnp.bfloat16),
        in_specs=[smem, vmem, vmem, vmem],
        out_specs=vmem,
        compiler_params=params,
        cost_estimate=pl.CostEstimate(flops=2 * 128 * width * head, bytes_accessed=2 << 20, transcendentals=0),
    )(place, activations, own, other)
    return values_out, weight_grad


def solution(mesh):
    fine = Mesh(mesh.devices.reshape(Y, ZH, X, ZL, CORE), AXES)
    tokens, local = P(AXES, None), ("zl", "core")
    return jax.shard_map(
        on_device,
        mesh=fine,
        in_specs=(tokens, P(local, None, None), P(local, None), tokens),
        out_specs=(tokens, tokens),
        check_vma=False,
    )
```

```python
import jax
import jax.numpy as jnp
from jax import lax
from jax.experimental import pallas as pl
from jax.experimental.pallas import tpu as pltpu
from jax.sharding import Mesh, PartitionSpec as P

Y, ZH, X, ZL, CORE = 8, 2, 4, 8, 2
AXES = ("y", "zh", "x", "zl", "core")
FIRST, SECOND = 3, 1


def term_kernel(scale, core_ref, act_ref, cot_ref, keep_ref, send_ref):
    first = core_ref[0] == 0
    share = 4
    per = act_ref.shape[1] // (Y * ZH)
    sub = per // X
    half = sub // 2
    cot = cot_ref[...]
    low = lax.broadcasted_iota(jnp.int32, (sub // 16, 8, cot.shape[1]), 1) < share
    for outer in range(Y * ZH):
        part = lax.dot_general(
            act_ref[:, outer * per : (outer + 1) * per],
            cot,
            (((0,), (0,)), ((), ())),
            preferred_element_type=jnp.float32,
        )
        part = part * scale
        for x in range(X):
            tiles = part[x * sub : (x + 1) * sub].reshape(sub // 16, 2, 8, cot.shape[1])
            even, odd = tiles[:, 0], tiles[:, 1]
            zero = jnp.where(low, even, pltpu.roll(odd, share, 1))
            one = jnp.where(low, pltpu.roll(even, share, 1), odd)
            at = pl.ds(((outer // ZH * X + x) * ZH + outer % ZH) * half, half)
            keep_ref[at, :] = jnp.where(first, zero, one).reshape(half, -1)
            send_ref[at, :] = jnp.where(first, one, zero).reshape(half, -1).astype(send_ref.dtype)


def gather_order():
    held = [0, FIRST, -FIRST]
    return held + [step + SECOND for step in held] + [step - SECOND for step in held[:2]]


def project(place_ref, act_ref, shards_ref, which):
    zl = place_ref[0]
    steps = gather_order()
    block = shards_ref.shape[0] // len(steps)
    total = None
    for place, step in enumerate(steps):
        at = pl.multiple_of((2 * ((zl + step + ZL) % ZL) + which) * block, block)
        piece = jnp.dot(
            act_ref[:, pl.ds(at, block)],
            shards_ref[pl.ds(place * block, block), :],
            preferred_element_type=jnp.float32,
        )
        total = piece if total is None else total + piece
    return total


def own_kernel(place_ref, act_ref, own_ref, out_ref):
    out_ref[...] = project(place_ref, act_ref, own_ref, place_ref[1])


def other_kernel(place_ref, act_ref, other_ref, part_ref, out_ref):
    total = part_ref[...] + project(place_ref, act_ref, other_ref, 1 - place_ref[1])
    out_ref[...] = total.astype(out_ref.dtype)


def along_z(value, shift):
    ring = ZH * ZL
    pairs = [((z + shift) % ring, z) for z in range(ring)]
    return lax.ppermute(value, ("zh", "zl"), pairs)


def on_device(activations, codes, scales, cotangent):
    width = activations.shape[1]
    head = cotangent.shape[1]
    tokens = activations.shape[0] * Y * ZH * X * ZL * CORE
    vmem = pl.BlockSpec(memory_space=pltpu.VMEM)
    smem = pl.BlockSpec(memory_space=pltpu.SMEM)
    params = pltpu.CompilerParams(vmem_limit_bytes=32 * 1024 * 1024)
    core = lax.axis_index("core").reshape(1).astype(jnp.int32)
    place = jnp.concatenate([lax.axis_index("zl").reshape(1).astype(jnp.int32), core])
    swap = [(0, 1), (1, 0)]

    stored = (codes.astype(jnp.float32) * scales[:, None, :]).astype(jnp.bfloat16)
    own = stored.reshape(-1, head)

    rows = width // CORE
    keep, send = pl.pallas_call(
        lambda *refs: term_kernel(float(tokens) ** (-0.5), *refs),
        out_shape=[
            jax.ShapeDtypeStruct((rows, head), jnp.float32),
            jax.ShapeDtypeStruct((rows, head), jnp.bfloat16),
        ],
        in_specs=[smem, vmem, vmem],
        out_specs=[vmem, vmem],
        compiler_params=params,
        cost_estimate=pl.CostEstimate(flops=2 * 128 * width * head, bytes_accessed=3 << 20, transcendentals=0),
    )(core, activations, cotangent)
    held = jnp.concatenate([own, along_z(own, FIRST), along_z(own, -FIRST)])
    chip = keep + lax.ppermute(send, "core", swap).astype(jnp.float32)
    chip = chip.astype(jnp.bfloat16)
    two = 2 * own.shape[0]
    own = jnp.concatenate([held, along_z(held, SECOND), along_z(held[:two], -SECOND)])
    got = lax.all_to_all(chip, ("y", "x"), 0, 0, tiled=True)
    peers = ZH * ZL
    line = got.reshape(Y * X, peers, rows // (Y * X * peers), head).astype(jnp.float32).sum(0)
    weight_grad = lax.all_to_all(line, ("zh", "zl"), 0, 0, tiled=True).sum(0)

    part = pl.pallas_call(
        own_kernel,
        out_shape=jax.ShapeDtypeStruct(cotangent.shape, jnp.float32),
        in_specs=[smem, vmem, vmem],
        out_specs=vmem,
        compiler_params=params,
        cost_estimate=pl.CostEstimate(flops=128 * width * head, bytes_accessed=1 << 20, transcendentals=0),
    )(place, activations, own)
    other = lax.ppermute(own, "core", swap)
    values_out = pl.pallas_call(
        other_kernel,
        out_shape=jax.ShapeDtypeStruct(cotangent.shape, jnp.bfloat16),
        in_specs=[smem, vmem, vmem, vmem],
        out_specs=vmem,
        compiler_params=params,
        cost_estimate=pl.CostEstimate(flops=128 * width * head, bytes_accessed=1 << 20, transcendentals=0),
    )(place, activations, other, part)
    return values_out, weight_grad


def solution(mesh):
    fine = Mesh(mesh.devices.reshape(Y, ZH, X, ZL, CORE), AXES)
    tokens, local = P(AXES, None), ("zl", "core")
    return jax.shard_map(
        on_device,
        mesh=fine,
        in_specs=(tokens, P(local, None, None), P(local, None), tokens),
        out_specs=(tokens, tokens),
        check_vma=False,
    )
```

```python
import jax
import jax.numpy as jnp
from jax import lax
from jax.experimental import pallas as pl
from jax.experimental.pallas import tpu as pltpu
from jax.sharding import Mesh, PartitionSpec as P

Y, ZH, X, ZL, CORE = 8, 2, 4, 8, 2
AXES = ("y", "zh", "x", "zl", "core")
FIRST, SECOND = 3, 1


def term_kernel(scale, core_ref, act_ref, cot_ref, keep_ref, send_ref):
    first = core_ref[0] == 0
    share = 4
    per = act_ref.shape[1] // (Y * ZH)
    sub = per // X
    half = sub // 2
    cot = cot_ref[...]
    low = lax.broadcasted_iota(jnp.int32, (sub // 16, 8, cot.shape[1]), 1) < share
    for outer in range(Y * ZH):
        part = lax.dot_general(
            act_ref[:, outer * per : (outer + 1) * per],
            cot,
            (((0,), (0,)), ((), ())),
            preferred_element_type=jnp.float32,
        )
        part = part * scale
        for x in range(X):
            tiles = part[x * sub : (x + 1) * sub].reshape(sub // 16, 2, 8, cot.shape[1])
            even, odd = tiles[:, 0], tiles[:, 1]
            zero = jnp.where(low, even, pltpu.roll(odd, share, 1))
            one = jnp.where(low, pltpu.roll(even, share, 1), odd)
            at = pl.ds(((outer // ZH * X + x) * ZH + outer % ZH) * half, half)
            keep_ref[at, :] = jnp.where(first, zero, one).reshape(half, -1)
            send_ref[at, :] = jnp.where(first, one, zero).reshape(half, -1).astype(send_ref.dtype)


def gather_order():
    held = [0, FIRST, -FIRST]
    return held + [step + SECOND for step in held] + [step - SECOND for step in held[:2]]


def project(place_ref, act_ref, shards_ref, which):
    zl = place_ref[0]
    steps = gather_order()
    block = shards_ref.shape[0] // len(steps)
    total = None
    for place, step in enumerate(steps):
        at = pl.multiple_of((2 * ((zl + step + ZL) % ZL) + which) * block, block)
        piece = jnp.dot(
            act_ref[:, pl.ds(at, block)],
            shards_ref[pl.ds(place * block, block), :],
            preferred_element_type=jnp.float32,
        )
        total = piece if total is None else total + piece
    return total


def own_kernel(place_ref, act_ref, own_ref, out_ref):
    out_ref[...] = project(place_ref, act_ref, own_ref, place_ref[1])


def other_kernel(place_ref, act_ref, other_ref, part_ref, out_ref):
    total = part_ref[...] + project(place_ref, act_ref, other_ref, 1 - place_ref[1])
    out_ref[...] = total.astype(out_ref.dtype)


def along_z(value, shift):
    ring = ZH * ZL
    pairs = [((z + shift) % ring, z) for z in range(ring)]
    return lax.ppermute(value, ("zh", "zl"), pairs)


def on_device(activations, codes, scales, cotangent):
    width = activations.shape[1]
    head = cotangent.shape[1]
    tokens = activations.shape[0] * Y * ZH * X * ZL * CORE
    vmem = pl.BlockSpec(memory_space=pltpu.VMEM)
    smem = pl.BlockSpec(memory_space=pltpu.SMEM)
    params = pltpu.CompilerParams(vmem_limit_bytes=32 * 1024 * 1024)
    core = lax.axis_index("core").reshape(1).astype(jnp.int32)
    place = jnp.concatenate([lax.axis_index("zl").reshape(1).astype(jnp.int32), core])
    swap = [(0, 1), (1, 0)]

    stored = (codes.astype(jnp.float32) * scales[:, None, :]).astype(jnp.bfloat16)
    own = stored.reshape(-1, head)

    cotangent, _ = lax.optimization_barrier((cotangent, stored))
    rows = width // CORE
    keep, send = pl.pallas_call(
        lambda *refs: term_kernel(float(tokens) ** (-0.5), *refs),
        out_shape=[
            jax.ShapeDtypeStruct((rows, head), jnp.float32),
            jax.ShapeDtypeStruct((rows, head), jnp.bfloat16),
        ],
        in_specs=[smem, vmem, vmem],
        out_specs=[vmem, vmem],
        compiler_params=params,
        cost_estimate=pl.CostEstimate(flops=2 * 128 * width * head, bytes_accessed=3 << 20, transcendentals=0),
    )(core, activations, cotangent)
    held = jnp.concatenate([own, along_z(own, FIRST), along_z(own, -FIRST)])
    chip = keep + lax.ppermute(send, "core", swap).astype(jnp.float32)
    chip = chip.astype(jnp.bfloat16)
    two = 2 * own.shape[0]
    own = jnp.concatenate([held, along_z(held, SECOND), along_z(held[:two], -SECOND)])
    got = lax.all_to_all(chip, ("y", "x"), 0, 0, tiled=True)
    peers = ZH * ZL
    line = got.reshape(Y * X, peers, rows // (Y * X * peers), head).astype(jnp.float32).sum(0)
    weight_grad = lax.all_to_all(line, ("zh", "zl"), 0, 0, tiled=True).sum(0)

    part = pl.pallas_call(
        own_kernel,
        out_shape=jax.ShapeDtypeStruct(cotangent.shape, jnp.float32),
        in_specs=[smem, vmem, vmem],
        out_specs=vmem,
        compiler_params=params,
        cost_estimate=pl.CostEstimate(flops=128 * width * head, bytes_accessed=1 << 20, transcendentals=0),
    )(place, activations, own)
    other = lax.ppermute(own, "core", swap)
    values_out = pl.pallas_call(
        other_kernel,
        out_shape=jax.ShapeDtypeStruct(cotangent.shape, jnp.bfloat16),
        in_specs=[smem, vmem, vmem, vmem],
        out_specs=vmem,
        compiler_params=params,
        cost_estimate=pl.CostEstimate(flops=128 * width * head, bytes_accessed=1 << 20, transcendentals=0),
    )(place, activations, other, part)
    return values_out, weight_grad


def solution(mesh):
    fine = Mesh(mesh.devices.reshape(Y, ZH, X, ZL, CORE), AXES)
    tokens, local = P(AXES, None), ("zl", "core")
    return jax.shard_map(
        on_device,
        mesh=fine,
        in_specs=(tokens, P(local, None, None), P(local, None), tokens),
        out_specs=(tokens, tokens),
        check_vma=False,
    )
```
